32 devices in a mesh: groups: 2 (over x), seq: 16 (over z, y, core).
Axes of the slice: x: 2, y: 2, z: 4, core: 2. Of those that a mesh axis runs over, the one named last changes fastest.
Arguments:
- tokens: bfloat16 [4096, 8192], P(('groups', 'seq')), parts along dimension 0, may hold values from -6 to 6
- request_adapters: int32 [32, 4], P(('groups', 'seq')), parts along dimension 0, may hold values from 0 to 1023
- prompt_token_count: int32 [32, 4], P(('groups', 'seq')), parts along dimension 0, may hold values from 1 to 48, 128 in all within a row
- adapter_slot_index: int32 [1024], replicated, may hold values from 0 to 1023, each once
- down_factor_shard: bfloat16 [16, 512, 65536], P('seq'), may hold values from -0.0625 to 0.0625
- up_factor_shard: bfloat16 [16, 512, 4096], P('seq'), may hold values from -0.75 to 0.75
- shared_key_weight: bfloat16 [8192, 512], P('seq'), may hold values from -0.0625 to 0.0625
Outputs:
- keys: bfloat16 [4096, 512], P(('groups', 'seq')), parts along dimension 0
The draws below stay inside these ranges and needn't reach their ends.
There are 2 independent parts, one for each index of `groups`. The reference program is written for one: setup_inputs(seed, part) draws one part's arguments, and reference() takes and returns one part's arrays. A program takes and returns all parts, laid end to end along the dimension named above; an argument that names none is the same for every part. Nothing has to cross between parts.
Inputs may be any that keep to these rules, and one draw needn't show every extreme that they name: `prompt_token_count`: the counts of one device sum to 128. `adapter_slot_index`: each slot once.
All inputs are finite; a program needn't handle non-finite values.
Results may differ from the reference program's by a relative error of at most 0.0043.
Values may be sent and summed in bfloat16 or wider, within the bound.
A program may use at most 256 MiB of HBM per device.

```python
import math
import jax
import jax.numpy as jnp
import numpy as np
from jax import lax

MODEL_WIDTH = 8192
KEY_FEATURES = 512
ADAPTER_RANK = 64
ADAPTERS = 1024
OWNER_GROUPS = 2
TOK_DEV = 128
REQ_DEV = 4
MAXLEN = 48
TOKENS = 2048
OWNER_DEVICES = 8
SLOTS_PER_OWNER = 512
N_SEQ = 16


def touch_ends(values, own_key, low, largest):
    place = [jax.random.randint(jax.random.fold_in(own_key, axis), (), 0, length) for axis, length in enumerate(values.shape)]
    main_axis = values.shape.index(max(values.shape))
    next_to = place[:main_axis] + [(place[main_axis] + 1) % values.shape[main_axis]] + place[main_axis + 1:]
    return values.at[tuple(place)].set(low).at[tuple(next_to)].set(largest)


def block_levels(own_key, extent, pieces, low, high):
    gain = 1.0
    for dim, blocks in pieces:
        heights = jax.random.uniform(jax.random.fold_in(jax.random.fold_in(own_key, 6), dim), (blocks,), jnp.float32, low / len(pieces), high / len(pieces))
        gain = gain * jnp.repeat(jnp.exp(heights), extent[dim] // blocks).reshape((-1,) + (1,) * (len(extent) - 1 - dim))
    return gain


def rank_bounds(number_of, slope):
    loads = [(1 << 20) // math.isqrt(rank ** slope) + 1 for rank in range(1, number_of + 1)]
    width = 1 + sum(loads) // (1 << 30)
    return np.cumsum(np.array([max(1, weight // width) for weight in loads]))


def ranked(key, extent, amount, lean):
    grid = rank_bounds(amount, lean)
    pick = jax.random.randint(jax.random.fold_in(key, 1), extent, 0, int(grid[amount - 1]))
    rank = jnp.searchsorted(jnp.asarray(grid, jnp.int32), pick, side="right")
    return jax.random.permutation(jax.random.fold_in(key, 2), amount)[rank].astype(jnp.int32)


def profile(count, total, bound, skew):
    weights = [(1 << 20) // math.isqrt(grade ** skew) + 1 for grade in range(2, count + 1)]
    surplus, counts = total - bound - (count - 1), [1] * (count - 1)
    while surplus > 0:
        candidates = [i for i in range(count - 1) if counts[i] < bound]
        pool, left = sum([weights[i] for i in candidates]), surplus
        for i in candidates:
            extra = min(bound - counts[i], max(1, left * weights[i] // pool), surplus)
            counts[i] = counts[i] + extra
            surplus = surplus - extra
    return np.array([bound] + counts)


def uneven(rng, amount, total, bound, slope):
    if amount == 2:
        one = jax.random.randint(rng, (), max(1, total - bound), min(bound, total - 1) + 1)
        return jnp.stack([one, total - one])
    sizes = jnp.asarray(profile(amount, total, bound, slope), jnp.int32)
    couples = (amount - 1) // 2
    source_of, taker = sizes[1:1 + 2 * couples:2], sizes[2:2 + 2 * couples:2]
    slack = jnp.minimum(source_of - 1, bound - taker)
    moved = jax.random.randint(jax.random.fold_in(rng, 1), (couples,), 0, 1 << 20) % (slack + 1)
    sizes = sizes.at[1:1 + 2 * couples:2].set(source_of - moved).at[2:2 + 2 * couples:2].set(taker + moved)
    return sizes[jax.random.permutation(jax.random.fold_in(rng, 2), amount)]


def scatter_about(stream_key, shape, scale, limit, shards=(), dtype=jnp.bfloat16):
    values = scale * jax.random.normal(stream_key, shape, jnp.float32)
    if shards:
        values = values * block_levels(stream_key, shape, shards, -0.22, 0.18)
    return jnp.clip(values, -limit, limit).astype(dtype)


def setup_inputs(seed: int = 0, part: int = 0) -> dict:
    splits = jax.random.split(jax.random.key(seed), 8)
    part_splits = jax.random.split(jax.random.fold_in(splits[7], part), 8)
    return {
        "tokens": scatter_about(part_splits[0], (TOKENS, MODEL_WIDTH), 1.0, 6.0, ((0, 16),)),
        "request_adapters": touch_ends(ranked(part_splits[1], (N_SEQ, REQ_DEV), ADAPTERS, 2), jax.random.fold_in(part_splits[1], 3), 0, ADAPTERS - 1).astype(jnp.int32),
        "prompt_token_count": jax.vmap(lambda own: uneven(own, REQ_DEV, TOK_DEV, MAXLEN, 2))(jax.random.split(part_splits[2], N_SEQ)).reshape((N_SEQ, REQ_DEV)).astype(jnp.int32),
        "adapter_slot_index": jax.random.permutation(splits[3], ADAPTERS).astype(jnp.int32),
        "down_factor_shard": scatter_about(splits[4], (N_SEQ, SLOTS_PER_OWNER, MODEL_WIDTH * ADAPTER_RANK // OWNER_DEVICES), MODEL_WIDTH ** -0.5, 0.0625, ((0, 16),)),
        "up_factor_shard": scatter_about(splits[5], (N_SEQ, SLOTS_PER_OWNER, ADAPTER_RANK * KEY_FEATURES // OWNER_DEVICES), ADAPTER_RANK ** -0.5, 0.75, ((0, 16),)),
        "shared_key_weight": scatter_about(splits[6], (MODEL_WIDTH, KEY_FEATURES), MODEL_WIDTH ** -0.5, 0.0625, ((0, 16),)),
    }


def reference(tokens, request_adapters, prompt_token_count, adapter_slot_index, down_factor_shard, up_factor_shard, shared_key_weight):
    tok_all = tokens.reshape(N_SEQ, TOK_DEV, MODEL_WIDTH)
    down_factor_store = down_factor_shard.reshape(OWNER_GROUPS, OWNER_DEVICES, SLOTS_PER_OWNER, MODEL_WIDTH * ADAPTER_RANK // OWNER_DEVICES)
    up_factor_store = up_factor_shard.reshape(OWNER_GROUPS, OWNER_DEVICES, SLOTS_PER_OWNER, ADAPTER_RANK * KEY_FEATURES // OWNER_DEVICES)

    def owner_rows(packed):
        rows_here, ids_here, counts_here = packed
        slots = adapter_slot_index[ids_here]
        halves = (slots // SLOTS_PER_OWNER).astype(jnp.int32)
        inner = (slots % SLOTS_PER_OWNER).astype(jnp.int32)
        seg_ends = jnp.cumsum(counts_here)
        positions = jnp.arange(TOK_DEV)
        owner_req = jnp.sum((positions[:, None] >= seg_ends[None, :]).astype(jnp.int32), axis=1)
        member = owner_req[:, None] == jnp.arange(REQ_DEV)[None, :]
        panels = down_factor_store[halves, :, inner, :].reshape(REQ_DEV, MODEL_WIDTH, ADAPTER_RANK).astype(jnp.float32)
        shrunk_all = jnp.einsum("td,qdr->tqr", rows_here.astype(jnp.float32), panels)
        shrunk = jnp.sum(jnp.where(member[:, :, None], shrunk_all, jnp.float32(0.0)), axis=1)
        shrunk_b = shrunk.astype(jnp.bfloat16)
        spread = jnp.where(member[:, :, None], shrunk_b[:, None, :], jnp.zeros((), jnp.bfloat16))
        spread = spread.reshape(TOK_DEV, REQ_DEV * ADAPTER_RANK)
        expand = up_factor_store[halves, :, inner, :].reshape(REQ_DEV * ADAPTER_RANK, KEY_FEATURES)
        delta = jnp.dot(spread, expand, preferred_element_type=jnp.float32)
        base = jnp.dot(rows_here, shared_key_weight, preferred_element_type=jnp.float32)
        return (base + delta).astype(jnp.bfloat16)

    projected = lax.map(owner_rows, (tok_all, request_adapters, prompt_token_count))
    return projected.reshape(N_SEQ * TOK_DEV, KEY_FEATURES)
```

```python
import jax
import jax.numpy as jnp
from jax import lax
from jax.sharding import PartitionSpec as P

KEY_FEATURES = 512
ADAPTER_RANK = 64
OWNER_GROUPS = 2


def running(counts):
    at = jnp.arange(counts.shape[0])
    return jnp.sum(jnp.where(at[None, :] <= at[:, None], counts[None, :], 0), axis=1)


def request_of(ends, length):
    return jnp.sum((jnp.arange(length)[:, None] >= ends[None, :]).astype(jnp.int32), axis=1)


def on_device(
    tokens,
    request_adapters,
    prompt_token_count,
    adapter_slot_index,
    down_factor_shard,
    up_factor_shard,
    shared_key_weight,
):
    n = lax.axis_size("seq")
    rows, feats = tokens.shape
    reqs = request_adapters.shape[1]
    g = n // OWNER_GROUPS
    stripe = feats // g
    slots_here = down_factor_shard.shape[1]
    me = lax.axis_index("seq")
    mine = me // g
    halves = [list(range(h * g, h * g + g)) for h in range(OWNER_GROUPS)]
    mirror = [(j, (j + g) % n) for j in range(n)]

    def exchange(x):
        return lax.all_to_all(x, "seq", 0, 0, axis_index_groups=halves, tiled=True)

    facts = jnp.concatenate([request_adapters, prompt_token_count], axis=1)
    facts = lax.all_gather(facts, ("groups", "seq"), axis=0, tiled=True)
    tokens, shared_key_weight, facts = lax.optimization_barrier((tokens, shared_key_weight, facts))
    every_slot = jnp.take(adapter_slot_index, facts[:, :reqs])
    every_count = facts[:, reqs:]

    home = (jnp.arange(every_slot.shape[0]) // g) % OWNER_GROUPS
    crossing = jnp.where(every_slot // slots_here != home[:, None], every_count, 0)
    most = jnp.max(jnp.sum(crossing.reshape(-1, g * reqs), axis=1))

    first = lax.axis_index("groups") * n
    slots = lax.dynamic_slice_in_dim(every_slot, first, n, 0)
    counts = lax.dynamic_slice_in_dim(every_count, first, n, 0)

    half_rows = exchange(tokens.reshape(rows, g, stripe).transpose(1, 0, 2))

    even = [(2 * m, m) for m in range(g)] + [(2 * m + 1, g + m) for m in range(g)]
    odd = [(2 * m + 1, m) for m in range(g)] + [(2 * m, g + m) for m in range(g)]
    w_a = lax.ppermute(shared_key_weight, "seq", even)
    w_b = lax.ppermute(shared_key_weight, "seq", odd)
    w_lo = jnp.where(mine == 0, w_a, w_b)
    w_hi = jnp.where(mine == 0, w_b, w_a)

    offset = slots - mine * slots_here
    inside = (offset >= 0) & (offset < slots_here)
    offset = jnp.clip(offset, 0, slots_here - 1)
    picked_b = jnp.take(up_factor_shard[0], offset, axis=0)
    send_b = jnp.where(inside[..., None], picked_b, jnp.zeros((), picked_b.dtype))
    got_b = lax.all_to_all(send_b, "seq", 0, 0, tiled=True)

    own_at, far_at = mine * g, (1 - mine) * g
    offset_own = lax.dynamic_slice_in_dim(offset, own_at, g, 0).reshape(-1)
    offset_far = lax.dynamic_slice_in_dim(offset, far_at, g, 0).reshape(-1)
    panels_own = jnp.take(down_factor_shard[0], offset_own, axis=0)
    panels_far = jnp.take(down_factor_shard[0], offset_far, axis=0)

    own_counts = lax.dynamic_slice_in_dim(counts, own_at, g, 0)
    far_counts = lax.dynamic_slice_in_dim(counts, far_at, g, 0)
    own_inside = lax.dynamic_slice_in_dim(inside, own_at, g, 0)
    far_inside = lax.dynamic_slice_in_dim(inside, far_at, g, 0)
    total = g * rows

    own_flat = own_counts.reshape(-1)
    leaves = ~own_inside.reshape(-1)
    own_ends = running(own_flat)
    out_ends = running(jnp.where(leaves, own_flat, 0))
    row_req = request_of(own_ends, total)
    is_req = row_req[:, None] == jnp.arange(g * reqs)[None, :]
    shift = jnp.where(leaves, out_ends - own_ends, 2 * total)
    place = jnp.arange(total) + jnp.sum(jnp.where(is_req, shift[None, :], 0), axis=1)
    stays = is_req & own_inside.reshape(-1)[None, :]
    far_ends = running(jnp.where(far_inside, far_counts, 0).reshape(-1))

    def with_room(room):
        def branch(half_rows, w_lo, w_hi, panels_own, panels_far, place, stays, far_ends):
            flat = half_rows.reshape(total, stripe)
            chosen = place[None, :] == jnp.arange(room)[:, None]
            packed = jnp.dot(
                chosen.astype(jnp.bfloat16), flat, preferred_element_type=jnp.float32
            ).astype(jnp.bfloat16)
            came = lax.ppermute(packed, "seq", mirror)

            depth = w_lo.shape[0]
            base = jnp.dot(flat[:, :depth], w_lo, preferred_element_type=jnp.float32)
            base = base + jnp.dot(flat[:, depth:], w_hi, preferred_element_type=jnp.float32)
            base = exchange(base.astype(jnp.bfloat16).reshape(g, rows, KEY_FEATURES))
            base = jnp.sum(base.astype(jnp.float32), axis=0)

            p_own = panels_own.reshape(g, reqs, stripe, ADAPTER_RANK)
            keep = stays.reshape(g, rows, g, reqs)
            keep = jnp.sum(
                jnp.where(jnp.eye(g, dtype=bool)[:, None, :, None], keep, False), axis=2
            ).astype(bool)
            terms = jnp.einsum(
                "jtc,jqcr->jtqr", half_rows, p_own, preferred_element_type=jnp.float32
            )
            own = jnp.sum(jnp.where(keep[..., None], terms, 0.0), axis=2)

            p_far = panels_far.reshape(g * reqs, stripe, ADAPTER_RANK)
            step = room if room * g * reqs * ADAPTER_RANK <= (1 << 22) else rows
            req = request_of(far_ends, room)

            def far_terms(rows_in, req_in):
                terms = jnp.einsum(
                    "tc,qcr->tqr", rows_in, p_far, preferred_element_type=jnp.float32
                )
                hit = req_in[:, None] == jnp.arange(g * reqs)[None, :]
                return jnp.sum(jnp.where(hit[..., None], terms, 0.0), axis=1)

            if step == room:
                far = far_terms(came, req)
            else:
                far = lax.map(
                    lambda args: far_terms(*args),
                    (came.reshape(-1, step, stripe), req.reshape(-1, step)),
                ).reshape(room, ADAPTER_RANK)
            back = lax.ppermute(far, "seq", mirror)
            back = jnp.dot(
                chosen.astype(jnp.float32).T, back, precision=lax.Precision.HIGHEST
            )
            shrunk = own + back.reshape(g, rows, ADAPTER_RANK)
            shrunk = jnp.sum(exchange(shrunk), axis=0)
            return base, shrunk

        return branch

    unit = total // 16
    rooms = [unit * k for k in (8, 9, 10, 11, 12, 16)]
    which = sum((most > room).astype(jnp.int32) for room in rooms[:-1])
    base, shrunk = lax.switch(
        which,
        [with_room(room) for room in rooms],
        half_rows, w_lo, w_hi, panels_own, panels_far, place, stays, far_ends,
    )

    halves_b = jnp.sum(got_b.reshape(OWNER_GROUPS, g, reqs, got_b.shape[2]), axis=0)
    panels_b = halves_b.transpose(1, 0, 2).reshape(reqs * ADAPTER_RANK, KEY_FEATURES)
    member = request_of(running(prompt_token_count[0]), rows)[:, None] == jnp.arange(reqs)[None, :]
    shrunk_b = shrunk.astype(jnp.bfloat16)
    spread = jnp.where(member[:, :, None], shrunk_b[:, None, :], jnp.zeros((), jnp.bfloat16))
    spread = spread.reshape(rows, reqs * ADAPTER_RANK)
    delta = jnp.dot(spread, panels_b, preferred_element_type=jnp.float32)
    return (base + delta).astype(jnp.bfloat16)


def solution(mesh):
    in_specs = (
        P(("groups", "seq"), None),
        P(("groups", "seq"), None),
        P(("groups", "seq"), None),
        P(),
        P("seq", None, None),
        P("seq", None, None),
        P("seq", None),
    )
    out_specs = P(("groups", "seq"), None)
    return jax.shard_map(
        on_device, mesh=mesh, in_specs=in_specs, out_specs=out_specs, check_vma=False
    )
```

```python
import jax
import jax.numpy as jnp
from jax import lax
from jax.experimental import pallas as pl
from jax.experimental.pallas import tpu as pltpu
from jax.sharding import PartitionSpec as P

KEY_FEATURES = 512
ADAPTER_RANK = 64
OWNER_GROUPS = 2


def running(counts):
    at = jnp.arange(counts.shape[-1])
    return jnp.sum(jnp.where(at[None, :] <= at[:, None], counts[..., None, :], 0), axis=-1)


def share_kernel(parts, n, mine_ref, all_ref, send_sem, recv_sem):
    part, seat = lax.axis_index("groups"), lax.axis_index("seq")
    devices = parts * n
    me = part * n + seat
    barrier = pltpu.get_barrier_semaphore()

    def peer(k):
        to = lax.rem(me + k, devices)
        return (to // n, lax.rem(to, n))

    def greet(k, _):
        pl.semaphore_signal(barrier, inc=1, device_id=peer(k), device_id_type=pl.DeviceIdType.MESH)
        return 0

    lax.fori_loop(1, devices, greet, 0)
    at = pl.ds(pl.multiple_of(me * 8, 8), 8)
    all_ref[at, :] = mine_ref[...]
    pl.semaphore_wait(barrier, devices - 1)

    def copy(k):
        return pltpu.make_async_remote_copy(
            src_ref=mine_ref,
            dst_ref=all_ref.at[at, :],
            send_sem=send_sem.at[k],
            recv_sem=recv_sem.at[k],
            device_id=peer(k),
            device_id_type=pl.DeviceIdType.MESH,
        )

    def send(k, _):
        copy(k).start()
        return 0

    def finish(k, _):
        copy(k).wait()
        return 0

    lax.fori_loop(1, devices, send, 0)
    lax.fori_loop(1, devices, finish, 0)


def share(facts):
    parts, n = lax.axis_size("groups"), lax.axis_size("seq")
    width = facts.shape[0]
    block = jnp.pad(facts[None, :], ((0, 7), (0, 128 - width)))
    every = pl.pallas_call(
        lambda *refs: share_kernel(parts, n, *refs),
        out_shape=jax.ShapeDtypeStruct((parts * n * 8, 128), jnp.int32),
        in_specs=[pl.BlockSpec(memory_space=pltpu.VMEM)],
        out_specs=pl.BlockSpec(memory_space=pltpu.VMEM),
        scratch_shapes=[
            pltpu.SemaphoreType.DMA((parts * n,)),
            pltpu.SemaphoreType.DMA((parts * n,)),
        ],
        compiler_params=pltpu.CompilerParams(collective_id=0, has_side_effects=True),
        name="share_facts",
    )(block)
    return every.reshape(parts * n, 8, 128)[:, 0, :width]


def on_device(
    tokens,
    request_adapters,
    prompt_token_count,
    adapter_slot_index,
    down_factor_shard,
    up_factor_shard,
    shared_key_weight,
):
    n = lax.axis_size("seq")
    rows, feats = tokens.shape
    reqs = request_adapters.shape[1]
    g = n // OWNER_GROUPS
    stripe = feats // g
    total = g * rows
    unit = total // 16
    slots_here = down_factor_shard.shape[1]
    mine = lax.axis_index("seq") // g
    halves = [list(range(h * g, h * g + g)) for h in range(OWNER_GROUPS)]
    mirror = [(j, (j + g) % n) for j in range(n)]

    def exchange(x):
        return lax.all_to_all(x, "seq", 0, 0, axis_index_groups=halves, tiled=True)

    my_slots = jnp.take(adapter_slot_index, request_adapters[0])
    facts = share(jnp.concatenate([my_slots, prompt_token_count[0]]))
    split = tokens.reshape(rows, g, stripe).transpose(1, 0, 2)
    split, shared_key_weight, facts = lax.optimization_barrier((split, shared_key_weight, facts))
    every_slot, every_count = facts[:, :reqs], facts[:, reqs:]

    half_rows = exchange(split)

    home = (jnp.arange(every_slot.shape[0]) // g) % OWNER_GROUPS
    crossing = jnp.where(every_slot // slots_here != home[:, None], every_count, 0)
    most = jnp.max(jnp.sum(crossing.reshape(-1, g * reqs), axis=1))

    first = lax.axis_index("groups") * n
    own_at, far_at = first + mine * g, first + (1 - mine) * g

    def of_half(start):
        slots = lax.dynamic_slice_in_dim(every_slot, start, g, 0)
        counts = lax.dynamic_slice_in_dim(every_count, start, g, 0)
        offset = slots - mine * slots_here
        inside = (offset >= 0) & (offset < slots_here)
        return jnp.clip(offset, 0, slots_here - 1), inside, counts

    own_offset, own_inside, own_counts = of_half(own_at)
    far_offset, far_inside, far_counts = of_half(far_at)

    even = [(2 * m, m) for m in range(g)] + [(2 * m + 1, g + m) for m in range(g)]
    odd = [(2 * m + 1, m) for m in range(g)] + [(2 * m, g + m) for m in range(g)]
    w_a = lax.ppermute(shared_key_weight, "seq", even)
    w_b = lax.ppermute(shared_key_weight, "seq", odd)
    w_lo = jnp.where(mine == 0, w_a, w_b)
    w_hi = jnp.where(mine == 0, w_b, w_a)

    up = up_factor_shard[0]
    b_own = jnp.take(up, own_offset.reshape(-1), axis=0)
    b_far = lax.ppermute(jnp.take(up, far_offset.reshape(-1), axis=0), "seq", mirror)
    b_mine = jnp.where(own_inside.reshape(-1)[:, None], b_own, b_far)
    b_mine = b_mine.reshape(g, -1, KEY_FEATURES)

    at = jnp.arange(rows)[None, :, None]
    own_ends = running(own_counts)
    own_starts = own_ends - own_counts
    member = (at >= own_starts[:, None, :]) & (at < own_ends[:, None, :])
    leaving = jnp.where(own_inside, 0, own_counts).reshape(-1)
    out_starts = (running(leaving) - leaving).reshape(g, reqs)
    shift = jnp.where(own_inside, 2 * total, out_starts - own_starts)
    place = jnp.sum(jnp.where(member, at + shift[:, None, :], 0), axis=2).reshape(total)
    stays = member & own_inside[:, None, :]
    arriving = jnp.where(far_inside, far_counts, 0).reshape(-1)
    far_ends = running(arriving)
    far_starts = far_ends - arriving

    flat = half_rows.reshape(total, stripe)
    chosen = (place[None, :] == jnp.arange(total)[:, None]).astype(jnp.bfloat16)
    near, rest = 8 * unit, total - 8 * unit
    packed = jnp.dot(chosen[:near], flat, preferred_element_type=jnp.float32)
    came = lax.ppermute(packed.astype(jnp.bfloat16), "seq", mirror)
    packed_rest = jnp.dot(chosen[near:], flat, preferred_element_type=jnp.float32)
    packed_rest = packed_rest.astype(jnp.bfloat16)

    depth = w_lo.shape[0]
    base = jnp.dot(flat[:, :depth], w_lo, preferred_element_type=jnp.float32)
    base = base + jnp.dot(flat[:, depth:], w_hi, preferred_element_type=jnp.float32)
    base = base.astype(jnp.bfloat16).reshape(g, rows, KEY_FEATURES)
    got = exchange(jnp.concatenate([base, b_mine], axis=1))
    base = jnp.sum(got[:, :rows].astype(jnp.float32), axis=0)
    panels_b = got[:, rows:].reshape(g, reqs, -1, KEY_FEATURES).transpose(1, 0, 2, 3)
    panels_b = panels_b.reshape(reqs * ADAPTER_RANK, KEY_FEATURES)

    down = down_factor_shard[0]
    p_own = jnp.take(down, own_offset.reshape(-1), axis=0)
    p_own = p_own.reshape(g, reqs, stripe, ADAPTER_RANK)
    p_far = jnp.take(down, far_offset.reshape(-1), axis=0)
    p_far = p_far.reshape(g * reqs, stripe, ADAPTER_RANK)
    terms = jnp.einsum("jtc,jqcr->jtqr", half_rows, p_own, preferred_element_type=jnp.float32)
    own = jnp.sum(jnp.where(stays[..., None], terms, 0.0), axis=2)

    def far_terms(rows_in, start):
        spot = start + jnp.arange(rows_in.shape[0])[:, None]
        hit = (spot >= far_starts[None, :]) & (spot < far_ends[None, :])
        terms = jnp.einsum("tc,qcr->tqr", rows_in, p_far, preferred_element_type=jnp.float32)
        return jnp.sum(jnp.where(hit[..., None], terms, 0.0), axis=1).astype(jnp.bfloat16)

    def far_of(rows_in, start):
        if rows_in.shape[0] * g * reqs * ADAPTER_RANK <= (1 << 22):
            return far_terms(rows_in, start)
        blocks = rows_in.reshape(-1, rows, stripe)
        done = lax.map(
            lambda i: far_terms(blocks[i], start + i * rows), jnp.arange(blocks.shape[0])
        )
        return done.reshape(-1, ADAPTER_RANK)

    far = far_of(came, 0)
    back = lax.ppermute(far, "seq", mirror)

    def more(room):
        def branch(packed_rest):
            if room == 0:
                return jnp.zeros_like(packed_rest)
            sent = lax.ppermute(packed_rest[:room], "seq", mirror)
            return jnp.pad(sent, ((0, rest - room), (0, 0)))

        return branch

    rooms = [unit * k for k in (0, 1, 2, 3, 4, 8)]
    which = sum((most > near + room).astype(jnp.int32) for room in rooms[:-1])
    packed_rest, far = lax.optimization_barrier((packed_rest, far))
    came_rest = lax.switch(which, [more(room) for room in rooms], packed_rest)
    back_rest = lax.ppermute(far_of(came_rest, near), "seq", mirror)

    back = lax.dot_general(
        chosen[:near], back, (((0,), (0,)), ((), ())), preferred_element_type=jnp.float32
    )
    back = back + lax.dot_general(
        chosen[near:], back_rest, (((0,), (0,)), ((), ())), preferred_element_type=jnp.float32
    )
    shrunk = own + back.reshape(g, rows, ADAPTER_RANK)
    shrunk = jnp.sum(exchange(shrunk), axis=0)

    ends = running(prompt_token_count[0])
    at = jnp.arange(rows)[:, None]
    member = (at >= (ends - prompt_token_count[0])[None, :]) & (at < ends[None, :])
    shrunk_b = shrunk.astype(jnp.bfloat16)
    spread = jnp.where(member[:, :, None], shrunk_b[:, None, :], jnp.zeros((), jnp.bfloat16))
    spread = spread.reshape(rows, reqs * ADAPTER_RANK)
    delta = jnp.dot(spread, panels_b, preferred_element_type=jnp.float32)
    return (base + delta).astype(jnp.bfloat16)


def solution(mesh):
    in_specs = (
        P(("groups", "seq"), None),
        P(("groups", "seq"), None),
        P(("groups", "seq"), None),
        P(),
        P("seq", None, None),
        P("seq", None, None),
        P("seq", None),
    )
    out_specs = P(("groups", "seq"), None)
    return jax.shard_map(
        on_device, mesh=mesh, in_specs=in_specs, out_specs=out_specs, check_vma=False
    )
```

```python
import jax
import jax.numpy as jnp
from jax import lax
from jax.sharding import PartitionSpec as P

KEY_FEATURES = 512
ADAPTER_RANK = 64
OWNER_GROUPS = 2


def running(counts):
    at = jnp.arange(counts.shape[-1])
    return jnp.sum(jnp.where(at[None, :] <= at[:, None], counts[..., None, :], 0), axis=-1)


def share(facts):
    axes = ("groups", "seq")
    everyone = lax.axis_size("groups") * lax.axis_size("seq")
    copies = jnp.broadcast_to(facts[None, :], (everyone, facts.shape[0]))
    return lax.all_to_all(copies, axes, 0, 0, tiled=True)


def on_device(
    tokens,
    request_adapters,
    prompt_token_count,
    adapter_slot_index,
    down_factor_shard,
    up_factor_shard,
    shared_key_weight,
):
    n = lax.axis_size("seq")
    rows, feats = tokens.shape
    reqs = request_adapters.shape[1]
    g = n // OWNER_GROUPS
    stripe = feats // g
    total = g * rows
    unit = total // 16
    slots_here = down_factor_shard.shape[1]
    mine = lax.axis_index("seq") // g
    halves = [list(range(h * g, h * g + g)) for h in range(OWNER_GROUPS)]
    mirror = [(j, (j + g) % n) for j in range(n)]

    def exchange(x):
        return lax.all_to_all(x, "seq", 0, 0, axis_index_groups=halves, tiled=True)

    my_slots = jnp.take(adapter_slot_index, request_adapters[0])
    facts = share(jnp.concatenate([my_slots, prompt_token_count[0]]))
    tokens, shared_key_weight, facts = lax.optimization_barrier((tokens, shared_key_weight, facts))
    every_slot, every_count = facts[:, :reqs], facts[:, reqs:]

    half_rows = exchange(tokens.reshape(rows, g, stripe).transpose(1, 0, 2))

    home = (jnp.arange(every_slot.shape[0]) // g) % OWNER_GROUPS
    crossing = jnp.where(every_slot // slots_here != home[:, None], every_count, 0)
    most = jnp.max(jnp.sum(crossing.reshape(-1, g * reqs), axis=1))

    first = lax.axis_index("groups") * n
    own_at, far_at = first + mine * g, first + (1 - mine) * g

    def of_half(start):
        slots = lax.dynamic_slice_in_dim(every_slot, start, g, 0)
        counts = lax.dynamic_slice_in_dim(every_count, start, g, 0)
        offset = slots - mine * slots_here
        inside = (offset >= 0) & (offset < slots_here)
        return jnp.clip(offset, 0, slots_here - 1), inside, counts

    own_offset, own_inside, own_counts = of_half(own_at)
    far_offset, far_inside, far_counts = of_half(far_at)

    even = [(2 * m, m) for m in range(g)] + [(2 * m + 1, g + m) for m in range(g)]
    odd = [(2 * m + 1, m) for m in range(g)] + [(2 * m, g + m) for m in range(g)]
    w_a = lax.ppermute(shared_key_weight, "seq", even)
    w_b = lax.ppermute(shared_key_weight, "seq", odd)
    w_lo = jnp.where(mine == 0, w_a, w_b)
    w_hi = jnp.where(mine == 0, w_b, w_a)

    up = up_factor_shard[0]
    b_own = jnp.take(up, own_offset.reshape(-1), axis=0, mode="clip")
    b_far = lax.ppermute(jnp.take(up, far_offset.reshape(-1), axis=0, mode="clip"), "seq", mirror)
    b_mine = jnp.where(own_inside.reshape(-1)[:, None], b_own, b_far)
    b_mine = b_mine.reshape(g, -1, KEY_FEATURES)

    at = jnp.arange(rows)[None, :, None]
    own_ends = running(own_counts)
    own_starts = own_ends - own_counts
    member = (at >= own_starts[:, None, :]) & (at < own_ends[:, None, :])
    leaving = jnp.where(own_inside, 0, own_counts).reshape(-1)
    out_starts = (running(leaving) - leaving).reshape(g, reqs)
    shift = jnp.where(own_inside, 2 * total, out_starts - own_starts)
    place = jnp.sum(jnp.where(member, at + shift[:, None, :], 0), axis=2).reshape(total)
    stays = member & own_inside[:, None, :]
    arriving = jnp.where(far_inside, far_counts, 0).reshape(-1)
    far_ends = running(arriving)
    far_starts = far_ends - arriving

    flat = half_rows.reshape(total, stripe)
    chosen = (place[None, :] == jnp.arange(total)[:, None]).astype(jnp.bfloat16)
    near, rest = 8 * unit, total - 8 * unit
    packed = jnp.dot(chosen[:near], flat, preferred_element_type=jnp.float32)
    packed = packed.astype(jnp.bfloat16)
    packed_rest = jnp.dot(chosen[near:], flat, preferred_element_type=jnp.float32)
    packed_rest = packed_rest.astype(jnp.bfloat16)

    depth = w_lo.shape[0]
    base = jnp.dot(flat[:, :depth], w_lo, preferred_element_type=jnp.float32)
    base = base + jnp.dot(flat[:, depth:], w_hi, preferred_element_type=jnp.float32)
    base = base.astype(jnp.bfloat16).reshape(g, rows, KEY_FEATURES)
    got = exchange(jnp.concatenate([base, b_mine], axis=1))

    down = down_factor_shard[0]
    p_own = jnp.take(down, own_offset.reshape(-1), axis=0, mode="clip")
    p_far = jnp.take(down, far_offset.reshape(-1), axis=0, mode="clip")
    packed, p_own, p_far = lax.optimization_barrier((packed, p_own, p_far))
    came = lax.ppermute(packed, "seq", mirror)
    p_own = p_own.reshape(g, reqs, stripe, ADAPTER_RANK)
    p_far = p_far.reshape(g * reqs, stripe, ADAPTER_RANK)
    terms = jnp.einsum("jtc,jqcr->jtqr", half_rows, p_own, preferred_element_type=jnp.float32)
    own = jnp.sum(jnp.where(stays[..., None], terms, 0.0), axis=2)

    came, got, own, p_far = lax.optimization_barrier((came, got, own, p_far))
    def far_terms(rows_in, start):
        spot = start + jnp.arange(rows_in.shape[0])[:, None]
        hit = (spot >= far_starts[None, :]) & (spot < far_ends[None, :])
        terms = jnp.einsum("tc,qcr->tqr", rows_in, p_far, preferred_element_type=jnp.float32)
        return jnp.sum(jnp.where(hit[..., None], terms, 0.0), axis=1).astype(jnp.bfloat16)

    def far_of(rows_in, start):
        if rows_in.shape[0] * g * reqs * ADAPTER_RANK <= (1 << 22):
            return far_terms(rows_in, start)
        blocks = rows_in.reshape(-1, rows, stripe)
        done = lax.map(
            lambda i: far_terms(blocks[i], start + i * rows), jnp.arange(blocks.shape[0])
        )
        return done.reshape(-1, ADAPTER_RANK)

    far = far_of(came, 0)
    back = lax.ppermute(far, "seq", mirror)

    def more(room):
        def branch(packed_rest):
            if room == 0:
                return jnp.zeros_like(packed_rest)
            sent = lax.ppermute(packed_rest[:room], "seq", mirror)
            return jnp.pad(sent, ((0, rest - room), (0, 0)))

        return branch

    rooms = [unit * k for k in (0, 1, 2, 3, 4, 8)]
    which = sum((most > near + room).astype(jnp.int32) for room in rooms[:-1])
    packed_rest, far = lax.optimization_barrier((packed_rest, far))
    came_rest = lax.switch(which, [more(room) for room in rooms], packed_rest)
    back_rest = lax.ppermute(far_of(came_rest, near), "seq", mirror)

    back = lax.dot_general(
        chosen[:near], back, (((0,), (0,)), ((), ())), preferred_element_type=jnp.float32
    )
    back = back + lax.dot_general(
        chosen[near:], back_rest, (((0,), (0,)), ((), ())), preferred_element_type=jnp.float32
    )
    shrunk = own + back.reshape(g, rows, ADAPTER_RANK)
    shrunk = jnp.sum(exchange(shrunk), axis=0)

    base = jnp.sum(got[:, :rows].astype(jnp.float32), axis=0)
    panels_b = got[:, rows:].reshape(g, reqs, -1, KEY_FEATURES).transpose(1, 0, 2, 3)
    panels_b = panels_b.reshape(reqs * ADAPTER_RANK, KEY_FEATURES)
    ends = running(prompt_token_count[0])
    at = jnp.arange(rows)[:, None]
    member = (at >= (ends - prompt_token_count[0])[None, :]) & (at < ends[None, :])
    shrunk_b = shrunk.astype(jnp.bfloat16)
    spread = jnp.where(member[:, :, None], shrunk_b[:, None, :], jnp.zeros((), jnp.bfloat16))
    spread = spread.reshape(rows, reqs * ADAPTER_RANK)
    delta = jnp.dot(spread, panels_b, preferred_element_type=jnp.float32)
    return (base + delta).astype(jnp.bfloat16)


def solution(mesh):
    in_specs = (
        P(("groups", "seq"), None),
        P(("groups", "seq"), None),
        P(("groups", "seq"), None),
        P(),
        P("seq", None, None),
        P("seq", None, None),
        P("seq", None),
    )
    out_specs = P(("groups", "seq"), None)
    return jax.shard_map(
        on_device, mesh=mesh, in_specs=in_specs, out_specs=out_specs, check_vma=False
    )
```

```python
import jax
import jax.numpy as jnp
from jax import lax
from jax.sharding import PartitionSpec as P

KEY_FEATURES = 512
ADAPTER_RANK = 64
OWNER_GROUPS = 2


def running(counts):
    at = jnp.arange(counts.shape[-1])
    return jnp.sum(jnp.where(at[None, :] <= at[:, None], counts[..., None, :], 0), axis=-1)


def share(facts):
    axes = ("groups", "seq")
    everyone = lax.axis_size("groups") * lax.axis_size("seq")
    copies = jnp.broadcast_to(facts[None, :], (everyone, facts.shape[0]))
    return lax.all_to_all(copies, axes, 0, 0, tiled=True)


def on_device(
    tokens,
    request_adapters,
    prompt_token_count,
    adapter_slot_index,
    down_factor_shard,
    up_factor_shard,
    shared_key_weight,
):
    n = lax.axis_size("seq")
    rows, feats = tokens.shape
    reqs = request_adapters.shape[1]
    g = n // OWNER_GROUPS
    stripe = feats // g
    total = g * rows
    unit = total // 16
    slots_here = down_factor_shard.shape[1]
    mine = lax.axis_index("seq") // g
    halves = [list(range(h * g, h * g + g)) for h in range(OWNER_GROUPS)]
    mirror = [(j, (j + g) % n) for j in range(n)]

    def exchange(x):
        return lax.all_to_all(x, "seq", 0, 0, axis_index_groups=halves, tiled=True)

    my_slots = jnp.take(adapter_slot_index, request_adapters[0])
    facts = share(jnp.concatenate([my_slots, prompt_token_count[0]]))
    tokens, shared_key_weight, facts = lax.optimization_barrier((tokens, shared_key_weight, facts))
    every_slot, every_count = facts[:, :reqs], facts[:, reqs:]

    half_rows = exchange(tokens.reshape(rows, g, stripe).transpose(1, 0, 2))

    home = (jnp.arange(every_slot.shape[0]) // g) % OWNER_GROUPS
    crossing = jnp.where(every_slot // slots_here != home[:, None], every_count, 0)
    most = jnp.max(jnp.sum(crossing.reshape(-1, g * reqs), axis=1))

    first = lax.axis_index("groups") * n
    own_at, far_at = first + mine * g, first + (1 - mine) * g

    def of_half(start):
        slots = lax.dynamic_slice_in_dim(every_slot, start, g, 0)
        counts = lax.dynamic_slice_in_dim(every_count, start, g, 0)
        offset = slots - mine * slots_here
        inside = (offset >= 0) & (offset < slots_here)
        return jnp.clip(offset, 0, slots_here - 1), inside, counts

    own_offset, own_inside, own_counts = of_half(own_at)
    far_offset, far_inside, far_counts = of_half(far_at)

    even = [(2 * m, m) for m in range(g)] + [(2 * m + 1, g + m) for m in range(g)]
    odd = [(2 * m + 1, m) for m in range(g)] + [(2 * m, g + m) for m in range(g)]
    w_a = lax.ppermute(shared_key_weight, "seq", even)
    w_b = lax.ppermute(shared_key_weight, "seq", odd)
    w_lo = jnp.where(mine == 0, w_a, w_b)
    w_hi = jnp.where(mine == 0, w_b, w_a)

    up = up_factor_shard[0]
    b_own = jnp.take(up, own_offset.reshape(-1), axis=0, mode="clip")
    b_out = jnp.take(up, far_offset.reshape(-1), axis=0, mode="clip")
    b_far = lax.ppermute(b_out, "seq", mirror)

    at = jnp.arange(rows)[None, :, None]
    own_ends = running(own_counts)
    own_starts = own_ends - own_counts
    member = (at >= own_starts[:, None, :]) & (at < own_ends[:, None, :])
    leaving = jnp.where(own_inside, 0, own_counts).reshape(-1)
    out_starts = (running(leaving) - leaving).reshape(g, reqs)
    shift = jnp.where(own_inside, 2 * total, out_starts - own_starts)
    place = jnp.sum(jnp.where(member, at + shift[:, None, :], 0), axis=2).reshape(total)
    stays = member & own_inside[:, None, :]
    arriving = jnp.where(far_inside, far_counts, 0).reshape(-1)
    far_ends = running(arriving)
    far_starts = far_ends - arriving

    flat = half_rows.reshape(total, stripe)
    chosen = (place[None, :] == jnp.arange(total)[:, None]).astype(jnp.bfloat16)
    near, rest = 11 * unit, total - 11 * unit
    packed = jnp.dot(chosen[:near], flat, preferred_element_type=jnp.float32)
    packed = packed.astype(jnp.bfloat16)
    packed_rest = jnp.dot(chosen[near:], flat, preferred_element_type=jnp.float32)
    packed_rest = packed_rest.astype(jnp.bfloat16)

    down = down_factor_shard[0]
    p_own = jnp.take(down, own_offset.reshape(-1), axis=0, mode="clip")
    packed, flat, half_rows, far_offset, p_own, b_own, _ = lax.optimization_barrier(
        (packed, flat, half_rows, far_offset, p_own, b_own, b_out)
    )
    came = lax.ppermute(packed, "seq", mirror)
    b_mine = jnp.where(own_inside.reshape(-1)[:, None], b_own, b_far)
    b_mine = b_mine.reshape(g, -1, KEY_FEATURES)
    depth = w_lo.shape[0]
    base = jnp.dot(flat[:, :depth], w_lo, preferred_element_type=jnp.float32)
    base = base + jnp.dot(flat[:, depth:], w_hi, preferred_element_type=jnp.float32)
    base = base.astype(jnp.bfloat16).reshape(g, rows, KEY_FEATURES)
    got = exchange(jnp.concatenate([base, b_mine], axis=1))

    p_far = jnp.take(down, far_offset.reshape(-1), axis=0, mode="clip")
    p_own = p_own.reshape(g, reqs, stripe, ADAPTER_RANK)
    p_far = p_far.reshape(g * reqs, stripe, ADAPTER_RANK)
    terms = jnp.einsum("jtc,jqcr->jtqr", half_rows, p_own, preferred_element_type=jnp.float32)
    own = jnp.sum(jnp.where(stays[..., None], terms, 0.0), axis=2)

    came, got, own, p_far = lax.optimization_barrier((came, got, own, p_far))
    def far_terms(rows_in, start):
        spot = start + jnp.arange(rows_in.shape[0])[:, None]
        hit = (spot >= far_starts[None, :]) & (spot < far_ends[None, :])
        terms = jnp.einsum("tc,qcr->tqr", rows_in, p_far, preferred_element_type=jnp.float32)
        return jnp.sum(jnp.where(hit[..., None], terms, 0.0), axis=1).astype(jnp.bfloat16)

    def far_of(rows_in, start):
        if rows_in.shape[0] * g * reqs * ADAPTER_RANK <= (1 << 22):
            return far_terms(rows_in, start)
        blocks = rows_in.reshape(-1, rows, stripe)
        done = lax.map(
            lambda i: far_terms(blocks[i], start + i * rows), jnp.arange(blocks.shape[0])
        )
        return done.reshape(-1, ADAPTER_RANK)

    far = far_of(came, 0)
    back = lax.ppermute(far, "seq", mirror)

    def more(room):
        def branch(packed_rest):
            if room == 0:
                return jnp.zeros_like(packed_rest)
            sent = lax.ppermute(packed_rest[:room], "seq", mirror)
            return jnp.pad(sent, ((0, rest - room), (0, 0)))

        return branch

    rooms = [unit * k for k in (0, 1, 2, 5)]
    which = sum((most > near + room).astype(jnp.int32) for room in rooms[:-1])
    packed_rest, far = lax.optimization_barrier((packed_rest, far))
    came_rest = lax.switch(which, [more(room) for room in rooms], packed_rest)
    back_rest = lax.ppermute(far_of(came_rest, near), "seq", mirror)

    back = lax.dot_general(
        chosen[:near], back, (((0,), (0,)), ((), ())), preferred_element_type=jnp.float32
    )
    back = back + lax.dot_general(
        chosen[near:], back_rest, (((0,), (0,)), ((), ())), preferred_element_type=jnp.float32
    )
    shrunk = own + back.reshape(g, rows, ADAPTER_RANK)
    shrunk = jnp.sum(exchange(shrunk), axis=0)

    base = jnp.sum(got[:, :rows].astype(jnp.float32), axis=0)
    panels_b = got[:, rows:].reshape(g, reqs, -1, KEY_FEATURES).transpose(1, 0, 2, 3)
    panels_b = panels_b.reshape(reqs * ADAPTER_RANK, KEY_FEATURES)
    ends = running(prompt_token_count[0])
    at = jnp.arange(rows)[:, None]
    member = (at >= (ends - prompt_token_count[0])[None, :]) & (at < ends[None, :])
    shrunk_b = shrunk.astype(jnp.bfloat16)
    spread = jnp.where(member[:, :, None], shrunk_b[:, None, :], jnp.zeros((), jnp.bfloat16))
    spread = spread.reshape(rows, reqs * ADAPTER_RANK)
    delta = jnp.dot(spread, panels_b, preferred_element_type=jnp.float32)
    return (base + delta).astype(jnp.bfloat16)


def solution(mesh):
    in_specs = (
        P(("groups", "seq"), None),
        P(("groups", "seq"), None),
        P(("groups", "seq"), None),
        P(),
        P("seq", None, None),
        P("seq", None, None),
        P("seq", None),
    )
    out_specs = P(("groups", "seq"), None)
    return jax.shard_map(
        on_device, mesh=mesh, in_specs=in_specs, out_specs=out_specs, check_vma=False
    )
```
